32 devices in a mesh: ctx: 8 (over z, x), tp: 4 (over y, core).
Axes of the slice: x: 2, y: 2, z: 4, core: 2. Of those that a mesh axis runs over, the one named last changes fastest.
Arguments:
- query: bfloat16 [4096, 4096], P('ctx', 'tp'), may hold values from -6 to 6
- key_in: bfloat16 [4096, 4096], P('ctx', 'tp'), may hold values from -6 to 6
- value: bfloat16 [4096, 4096], P('ctx', 'tp'), may hold values from -6 to 6
- rates: float32 [256, 16], P('tp'), as said below
- residues: float32 [256, 16], P('tp'), as said below
- skip_gain: float32 [4096], P('tp'), may hold values from 0.5 to 1.5
- out_weight: bfloat16 [4096, 4096], P('tp'), may hold values from -0.09375 to 0.09375
Outputs:
- layer_out: bfloat16 [4096, 4096], P('ctx', 'tp')
The draws below stay inside these ranges and needn't reach their ends.
Inputs may be any that keep to these rules, and one draw needn't show every extreme that they name: `rates`: positive, at most 0.0625. `residues`: either sign.
All inputs are finite; a program needn't handle non-finite values.
Results may differ from the reference program's by a relative error of at most 0.0095.
Values may be sent and summed in bfloat16 or wider, within the bound.
No kernel may reach another device: no remote copies, remote signals or barrier semaphores. Data moves between devices by JAX's collectives and lax.ppermute only.
A program may use at most 128 MiB of HBM per device.

```python
import jax
import jax.numpy as jnp
from jax import lax

D = 4096
GROUP = 16
MODES = 16
TOK_DEV = 512
GROUPS = 256
SEQ = 4096
N_CTX = 8


def mode_table(key, ceiling):
    first, second = jax.random.split(jax.random.fold_in(key, 11))
    floor_rate = 0.5 / SEQ
    spread_draw = jax.random.uniform(first, (GROUPS, MODES), jnp.float32)
    rate_values = jnp.exp(jnp.log(floor_rate) + spread_draw * (jnp.log(ceiling) - jnp.log(floor_rate)))
    weights_drawn = jax.random.normal(second, (GROUPS, MODES), jnp.float32) * jnp.sqrt(2.0 * rate_values / MODES)
    return (rate_values, weights_drawn)


def draw_rates(key, part):
    ceiling = 0.0625
    return mode_table(key, ceiling)[0]


def draw_residues(key, part):
    ceiling = 0.0625
    return mode_table(key, ceiling)[1]


def level_of(key, shape, pieces, smallest, top_value):
    level, own = 1.0, jax.random.fold_in(key, 6)
    for position, blocks in pieces:
        heights = jnp.exp(jax.random.uniform(jax.random.fold_in(own, position), (blocks,), jnp.float32, smallest / len(pieces), top_value / len(pieces)))
        level = level * jnp.repeat(heights, shape[position] // blocks).reshape([-1 if axis == position else 1 for axis in range(len(shape))])
    return level


def centred(stream_key, shape, spread, reach, shards=(), held_as=jnp.bfloat16):
    entries = spread * jax.random.normal(stream_key, shape, jnp.float32)
    if shards:
        entries = entries * level_of(stream_key, shape, shards, -0.22, 0.18)
    return jnp.clip(entries, -reach, reach).astype(held_as)


def setup_inputs(seed: int = 0) -> dict:
    streams_of = jax.random.split(jax.random.key(seed), 8)
    return {
        "query": centred(streams_of[0], (SEQ, D), 1.0, 6.0, ((0, 8), (1, 4))),
        "key_in": centred(streams_of[1], (SEQ, D), 1.0, 6.0, ((0, 8), (1, 4))),
        "value": centred(streams_of[2], (SEQ, D), 1.0, 6.0, ((0, 8), (1, 4))),
        "rates": draw_rates(jax.random.fold_in(streams_of[7], 71), 0),
        "residues": draw_residues(jax.random.fold_in(streams_of[7], 71), 0),
        "skip_gain": jnp.clip(0.5 + 1.0 * jax.random.uniform(streams_of[5], (D,), jnp.float32) ** level_of(streams_of[5], (D,), ((0, 4),), -0.2, 0.2), 0.5, 1.5),
        "out_weight": centred(streams_of[6], (D, D), D ** -0.5, 0.09375, ((0, 4),)),
    }


def reference(query, key_in, value, rates, residues, skip_gain, out_weight):
    product_bf = (key_in.astype(jnp.float32) * value.astype(jnp.float32)).astype(jnp.bfloat16)
    signal = product_bf.astype(jnp.float32)
    groups_all = D // GROUP
    block_rows = TOK_DEV
    positions = jnp.arange(block_rows, dtype=jnp.float32)
    filter_local = jnp.sum(residues[:, :, None] * jnp.exp(-rates[:, :, None] * positions[None, None, :]), axis=1)
    lag_index = (jnp.arange(block_rows, dtype=jnp.int32)[:, None] - jnp.arange(block_rows, dtype=jnp.int32)[None, :]).astype(jnp.int32)
    toeplitz = jnp.where(lag_index[None] >= 0, jnp.take(filter_local, jnp.clip(lag_index, 0, block_rows - 1), axis=1), jnp.float32(0.0))
    rate_cols = jnp.repeat(rates, GROUP, axis=0).T
    residue_cols = jnp.repeat(residues, GROUP, axis=0).T
    decay_in = jnp.exp(-rate_cols[:, :, None] * (block_rows - 1.0 - positions)[None, None, :])
    decay_out = residue_cols[:, :, None] * jnp.exp(-rate_cols[:, :, None] * (positions + 1.0)[None, None, :])
    block_decay = jnp.exp(-rate_cols * block_rows)
    blocks_in = signal.reshape(N_CTX, block_rows, D)

    def advance(state, block):
        channel_first = block.T
        local = jnp.einsum("gts,gcs->gct", toeplitz, channel_first.reshape(groups_all, GROUP, block_rows), precision=lax.Precision.HIGHEST).reshape(D, block_rows)
        past = jnp.einsum("mct,mc->ct", decay_out, state, precision=lax.Precision.HIGHEST)
        summary = jnp.einsum("mcs,cs->mc", decay_in, channel_first, precision=lax.Precision.HIGHEST)
        return block_decay * state + summary, (local + past).T

    _, conv_blocks = lax.scan(advance, jnp.zeros((MODES, D), jnp.float32), blocks_in)
    conv = conv_blocks.reshape(signal.shape)
    mixed = (query.astype(jnp.float32) * (conv + skip_gain[None, :] * signal)).astype(jnp.bfloat16)
    return jnp.dot(mixed, out_weight, preferred_element_type=jnp.float32).astype(jnp.bfloat16)
```

```python
import jax
import jax.numpy as jnp
from jax import lax
from jax.experimental import pallas as pl
from jax.experimental.pallas import tpu as pltpu
from jax.sharding import PartitionSpec as P

GROUP = 16
LANES = 128
SUBS = 8
BLK = 256
SEG = 256
CHUNK = 128
F32, BF16 = jnp.float32, jnp.bfloat16


def split_bf16(x, parts):
    pieces = []
    for _ in range(parts):
        piece = x.astype(BF16)
        pieces.append(piece)
        x = x - piece.astype(F32)
    return pieces


def dot(a, b):
    return lax.dot_general(a, b, (((1,), (0,)), ((), ())), preferred_element_type=F32)


def group_mask(groups, modes, channels):
    shape = (groups, modes, channels)
    return lax.broadcasted_iota(jnp.int32, shape, 0) == (
        lax.broadcasted_iota(jnp.int32, shape, 2) // GROUP
    )


def column_of(table, modes):
    groups = table.shape[0]
    rows = groups * modes
    spread = jnp.broadcast_to(table[:, None, :], (groups, modes, modes)).reshape(rows, modes)
    pick = lax.broadcasted_iota(jnp.int32, (rows, modes), 1) == (
        lax.broadcasted_iota(jnp.int32, (rows, modes), 0) % modes
    )
    return jnp.sum(jnp.where(pick, spread, 0.0), axis=1, keepdims=True)


def summary_kernel(k_ref, v_ref, rates_ref, residues_ref, sum_ref, rate_ref, residue_ref, flat_ref):
    groups, modes = rates_ref.shape
    rows = groups * modes
    tokens, channels = k_ref.shape
    rate = column_of(rates_ref[...], modes)
    residue = column_of(residues_ref[...], modes)
    mask = group_mask(groups, modes, channels)

    def compact(dense):
        kept = jnp.where(mask, dense.reshape(groups, modes, channels), 0.0)
        return jnp.sum(kept, axis=0)

    def store(ref, table):
        for tile in range(channels // LANES):
            ref[tile * modes : (tile + 1) * modes, :] = table[:, tile * LANES : (tile + 1) * LANES]

    position = lax.broadcasted_iota(jnp.int32, (rows, SEG), 1).astype(F32)
    decay = split_bf16(jnp.exp(-rate * (SEG - 1.0 - position)), 3)
    carry = jnp.exp(-rate * float(SEG))
    dense = None
    for seg in range(tokens // SEG):
        part = slice(seg * SEG, (seg + 1) * SEG)
        u = (k_ref[part, :].astype(F32) * v_ref[part, :].astype(F32)).astype(BF16)
        here = dot(decay[2], u) + dot(decay[1], u) + dot(decay[0], u)
        dense = here if dense is None else dense * carry + here
    store(sum_ref, compact(dense))
    wide = jnp.broadcast_to(rate, (rows, channels))
    store(rate_ref, compact(wide))
    store(residue_ref, compact(jnp.broadcast_to(residue, (rows, channels))))
    diagonal = lax.broadcasted_iota(jnp.int32, (rows, rows), 0) == lax.broadcasted_iota(
        jnp.int32, (rows, rows), 1
    )
    flat_ref[...] = jnp.sum(
        jnp.where(diagonal, jnp.broadcast_to(rate, (rows, rows)), 0.0), axis=0, keepdims=True
    )


def summary_call(key_in, value, rates, residues):
    tokens, channels = key_in.shape
    modes = rates.shape[1]
    groups = BLK // GROUP
    tiles = BLK // LANES
    table = jax.ShapeDtypeStruct((channels // LANES * modes, LANES), F32)
    table_spec = pl.BlockSpec((tiles * modes, LANES), lambda b: (b, 0))
    return pl.pallas_call(
        summary_kernel,
        grid=(channels // BLK,),
        in_specs=[
            pl.BlockSpec((tokens, BLK), lambda b: (0, b)),
            pl.BlockSpec((tokens, BLK), lambda b: (0, b)),
            pl.BlockSpec((groups, modes), lambda b: (b, 0)),
            pl.BlockSpec((groups, modes), lambda b: (b, 0)),
        ],
        out_specs=[
            table_spec,
            table_spec,
            table_spec,
            pl.BlockSpec((1, groups * modes), lambda b: (0, b)),
        ],
        out_shape=[table, table, table, jax.ShapeDtypeStruct((1, channels // GROUP * modes), F32)],
        compiler_params=pltpu.CompilerParams(vmem_limit_bytes=16 << 20),
        cost_estimate=pl.CostEstimate(
            flops=2 * 3 * tokens * BLK * channels, bytes_accessed=4 * tokens * channels, transcendentals=0
        ),
        name="block_summary",
    )(key_in, value, rates, residues)


def local_kernel(modes, k_ref, v_ref, rate_ref, residue_ref, skip_ref, out_ref, u_ref, state_ref):
    tokens, channels = k_ref.shape
    tiles = channels // LANES

    @pl.when(pl.program_id(0) == 0)
    def _():
        state_ref[...] = jnp.zeros_like(state_ref)

    for tile in range(tiles):
        lanes = slice(tile * LANES, (tile + 1) * LANES)
        u = (k_ref[:, lanes].astype(F32) * v_ref[:, lanes].astype(F32)).astype(BF16)
        u_ref[tile * tokens : (tile + 1) * tokens, :] = u.astype(F32)
    decay = [jnp.exp(-rate_ref[pl.ds(m, tiles, stride=modes), :]) for m in range(modes)]
    residue = [residue_ref[pl.ds(m, tiles, stride=modes), :] for m in range(modes)]
    skip = skip_ref[...]

    def step(t, states):
        u = u_ref[pl.ds(t, tiles, stride=tokens), :]
        states = tuple(d * s + u for d, s in zip(decay, states))
        terms = [skip * u] + [r * s for r, s in zip(residue, states)]
        while len(terms) > 1:
            terms = [a + b for a, b in zip(terms[::2], terms[1::2])] + (
                [terms[-1]] if len(terms) % 2 else []
            )
        out_ref[pl.ds(t, tiles, stride=tokens), :] = terms[0]
        return states

    first = tuple(state_ref[m * tiles : (m + 1) * tiles, :] for m in range(modes))
    last = lax.fori_loop(0, tokens, step, first, unroll=4)
    for m in range(modes):
        state_ref[m * tiles : (m + 1) * tiles, :] = last[m]


def local_call(key_in, value, rate_table, residue_table, skip_tiles, modes):
    tokens, channels = key_in.shape
    tiles = channels // LANES
    whole = lambda j: (0, 0)
    return pl.pallas_call(
        lambda *refs: local_kernel(modes, *refs),
        grid=(tokens // CHUNK,),
        in_specs=[
            pl.BlockSpec((CHUNK, channels), lambda j: (j, 0)),
            pl.BlockSpec((CHUNK, channels), lambda j: (j, 0)),
            pl.BlockSpec(rate_table.shape, whole),
            pl.BlockSpec(residue_table.shape, whole),
            pl.BlockSpec(skip_tiles.shape, whole),
        ],
        out_specs=pl.BlockSpec((tiles * CHUNK, LANES), lambda j: (j, 0)),
        out_shape=jax.ShapeDtypeStruct((tokens * tiles, LANES), F32),
        scratch_shapes=[
            pltpu.VMEM((tiles * CHUNK, LANES), F32),
            pltpu.VMEM((modes * tiles, LANES), F32),
        ],
        compiler_params=pltpu.CompilerParams(vmem_limit_bytes=16 << 20),
        cost_estimate=pl.CostEstimate(
            flops=4 * modes * tokens * channels, bytes_accessed=8 * tokens * channels, transcendentals=0
        ),
        name="local_conv",
    )(key_in, value, rate_table, residue_table, skip_tiles)


def mix_kernel(first, modes, q_ref, local_ref, state_ref, residue_ref, flat_ref, out_ref):
    tokens, channels = q_ref.shape
    tiles = channels // LANES
    groups = channels // GROUP
    rows = groups * modes
    weighted = state_ref[...] * residue_ref[...]
    weighted = jnp.concatenate([weighted[i * modes : (i + 1) * modes] for i in range(tiles)], axis=1)
    spread = jnp.broadcast_to(weighted[None], (groups, modes, channels))
    spread = jnp.where(group_mask(groups, modes, channels), spread, 0.0).reshape(rows, channels)
    since = lax.broadcasted_iota(jnp.int32, (tokens, rows), 0).astype(F32) + (first + 1.0)
    decay_hi, decay_lo = split_bf16(jnp.exp(-flat_ref[...] * since), 2)
    state_hi, state_lo = split_bf16(spread, 2)
    past = dot(decay_lo, state_hi) + dot(decay_hi, state_lo) + dot(decay_hi, state_hi)
    for tile in range(tiles):
        lanes = slice(tile * LANES, (tile + 1) * LANES)
        conv = local_ref[tile * tokens : (tile + 1) * tokens, :] + past[:, lanes]
        out_ref[:, lanes] = (q_ref[:, lanes].astype(F32) * conv).astype(BF16)


def mix_call(chunk, query, local, state, residue_table, flat_rates, modes):
    channels = query.shape[1]
    blocks = channels // BLK
    tiles = BLK // LANES
    table_spec = pl.BlockSpec((tiles * modes, LANES), lambda b: (b, 0))
    return pl.pallas_call(
        lambda *refs: mix_kernel(chunk * CHUNK, modes, *refs),
        grid=(blocks,),
        in_specs=[
            pl.BlockSpec((CHUNK, BLK), lambda b: (chunk, b)),
            pl.BlockSpec((tiles * CHUNK, LANES), lambda b: (chunk * blocks + b, 0)),
            table_spec,
            table_spec,
            pl.BlockSpec((1, BLK // GROUP * modes), lambda b: (0, b)),
        ],
        out_specs=pl.BlockSpec((CHUNK, BLK), lambda b: (0, b)),
        out_shape=jax.ShapeDtypeStruct((CHUNK, channels), BF16),
        compiler_params=pltpu.CompilerParams(vmem_limit_bytes=16 << 20),
        cost_estimate=pl.CostEstimate(
            flops=2 * 3 * CHUNK * BLK * channels, bytes_accessed=8 * CHUNK * channels, transcendentals=0
        ),
        name="mix",
    )(query, local, state, residue_table, flat_rates)


def project_kernel(at_ref, own_ref, pair_ref, own_w_ref, pair_w_ref, out_ref):
    total = dot(own_ref[...], own_w_ref[...]) + dot(pair_ref[...], pair_w_ref[...])
    out_ref[...] = total.astype(out_ref.dtype)


def project_call(at, mixed, mixed_pair, weight, weight_pair, out_dtype):
    tokens, depth = mixed.shape
    width = weight_pair.shape[1]
    cols = 256
    steps = width // cols
    return pl.pallas_call(
        project_kernel,
        grid_spec=pltpu.PrefetchScalarGridSpec(
            num_scalar_prefetch=1,
            grid=(steps,),
            in_specs=[
                pl.BlockSpec((tokens, depth), lambda n, at: (0, 0)),
                pl.BlockSpec((tokens, depth), lambda n, at: (0, 0)),
                pl.BlockSpec((depth, cols), lambda n, at: (0, at[0] * steps + n)),
                pl.BlockSpec((depth, cols), lambda n, at: (0, n)),
            ],
            out_specs=pl.BlockSpec((tokens, cols), lambda n, at: (0, n)),
        ),
        out_shape=jax.ShapeDtypeStruct((tokens, width), out_dtype),
        compiler_params=pltpu.CompilerParams(vmem_limit_bytes=24 << 20),
        cost_estimate=pl.CostEstimate(
            flops=4 * tokens * depth * width,
            bytes_accessed=4 * depth * width + 4 * tokens * width,
            transcendentals=0,
        ),
        name="project",
    )(at, mixed, mixed_pair, weight, weight_pair)


def start_state(summary, rate_table, block_rows, count):
    radix = 8

    def earlier(x, distance):
        return lax.ppermute(x, "ctx", [(i, i + distance) for i in range(count - distance)])

    def decayed(blocks):
        return jnp.exp(-rate_table * float(block_rows * blocks))

    total = jnp.zeros_like(summary)
    for distance in range(1, min(radix, count - 1) + 1):
        total = total + decayed(distance - 1) * earlier(summary, distance)
    span = radix
    while span < count - 1:
        base = total
        for step in range(1, radix):
            if step * span < count - 1:
                total = total + decayed(step * span) * earlier(base, step * span)
        span *= radix
    return total


def shards(query, key_in, value, rates, residues, skip_gain, out_weight, *, n_ctx, n_tp):
    tokens, channels = query.shape
    modes = rates.shape[1]
    width = out_weight.shape[1] // n_tp
    me = lax.axis_index("tp")

    def swap(x, bit):
        return lax.ppermute(x, "tp", [(i, i ^ bit) for i in range(n_tp)])

    def part_of_weight(at):
        return lax.dynamic_slice(out_weight, (0, at * width), (channels, width))

    summary, rate_table, residue_table, flat_rates = summary_call(key_in, value, rates, residues)
    pair_far = swap(part_of_weight(me ^ 3), 1)
    pair_near = swap(part_of_weight(me ^ 1), 1)
    state = start_state(summary, rate_table, tokens, n_ctx)
    skip_tiles = skip_gain.reshape(channels // LANES, LANES)
    local = local_call(key_in, value, rate_table, residue_table, skip_tiles, modes)

    far = (me ^ 2).reshape(1).astype(jnp.int32)
    near = me.reshape(1).astype(jnp.int32)
    mixed, mixed_pair, arrived = [], [], []
    for chunk in range(tokens // CHUNK):
        own = mix_call(chunk, query, local, state, residue_table, flat_rates, modes)
        other = swap(own, 1)
        partial = project_call(far, own, other, out_weight, pair_far, BF16)
        arrived.append(swap(partial, 2))
        mixed.append(own)
        mixed_pair.append(other)
    own_sum = project_call(
        near,
        jnp.concatenate(mixed, axis=0),
        jnp.concatenate(mixed_pair, axis=0),
        out_weight,
        pair_near,
        F32,
    )
    return (own_sum + jnp.concatenate(arrived, axis=0).astype(F32)).astype(BF16)


def solution(mesh):
    n_ctx, n_tp = mesh.shape["ctx"], mesh.shape["tp"]
    in_specs = (
        P("ctx", "tp"),
        P("ctx", "tp"),
        P("ctx", "tp"),
        P("tp", None),
        P("tp", None),
        P("tp"),
        P("tp", None),
    )

    def body(*args):
        return shards(*args, n_ctx=n_ctx, n_tp=n_tp)

    return jax.shard_map(body, mesh=mesh, in_specs=in_specs, out_specs=P("ctx", "tp"), check_vma=False)
```

```python
import jax
import jax.numpy as jnp
from jax import lax
from jax.experimental import pallas as pl
from jax.experimental.pallas import tpu as pltpu
from jax.sharding import PartitionSpec as P

GROUP = 16
LANES = 128
SUBS = 8
BLK = 256
SEG = 256
CHUNK = 128
F32, BF16 = jnp.float32, jnp.bfloat16


def split_bf16(x, parts):
    pieces = []
    for _ in range(parts):
        piece = x.astype(BF16)
        pieces.append(piece)
        x = x - piece.astype(F32)
    return pieces


def dot(a, b):
    return lax.dot_general(a, b, (((1,), (0,)), ((), ())), preferred_element_type=F32)


def group_mask(groups, modes, channels):
    shape = (groups, modes, channels)
    return lax.broadcasted_iota(jnp.int32, shape, 0) == (
        lax.broadcasted_iota(jnp.int32, shape, 2) // GROUP
    )


def column_of(table, modes):
    groups = table.shape[0]
    rows = groups * modes
    spread = jnp.broadcast_to(table[:, None, :], (groups, modes, modes)).reshape(rows, modes)
    pick = lax.broadcasted_iota(jnp.int32, (rows, modes), 1) == (
        lax.broadcasted_iota(jnp.int32, (rows, modes), 0) % modes
    )
    return jnp.sum(jnp.where(pick, spread, 0.0), axis=1, keepdims=True)


def summary_block(first, k_ref, v_ref, rates_ref, residues_ref, sum_ref, rate_ref, residue_ref, flat_ref):
    modes = rates_ref.shape[1]
    tokens, channels = k_ref.shape[0], BLK
    groups = channels // GROUP
    rows = groups * modes
    here_lanes = slice(first, first + channels)
    here_groups = slice(first // GROUP, first // GROUP + groups)
    rate = column_of(rates_ref[here_groups, :], modes)
    residue = column_of(residues_ref[here_groups, :], modes)
    mask = group_mask(groups, modes, channels)
    tile0 = first // LANES

    def compact(dense):
        kept = jnp.where(mask, dense.reshape(groups, modes, channels), 0.0)
        return jnp.sum(kept, axis=0)

    def store(ref, table):
        for tile in range(channels // LANES):
            rows_here = slice((tile0 + tile) * modes, (tile0 + tile + 1) * modes)
            ref[rows_here, :] = table[:, tile * LANES : (tile + 1) * LANES]

    position = lax.broadcasted_iota(jnp.int32, (rows, SEG), 1).astype(F32)
    decay = split_bf16(jnp.exp(-rate * (SEG - 1.0 - position)), 3)
    carry = jnp.exp(-rate * float(SEG))
    dense = None
    for seg in range(tokens // SEG):
        part = slice(seg * SEG, (seg + 1) * SEG)
        u = (k_ref[part, here_lanes].astype(F32) * v_ref[part, here_lanes].astype(F32)).astype(BF16)
        here = dot(decay[2], u) + dot(decay[1], u) + dot(decay[0], u)
        dense = here if dense is None else dense * carry + here
    store(sum_ref, compact(dense))
    wide = jnp.broadcast_to(rate, (rows, channels))
    store(rate_ref, compact(wide))
    store(residue_ref, compact(jnp.broadcast_to(residue, (rows, channels))))
    diagonal = lax.broadcasted_iota(jnp.int32, (rows, rows), 0) == lax.broadcasted_iota(
        jnp.int32, (rows, rows), 1
    )
    flat_ref[:, first // GROUP * modes : first // GROUP * modes + rows] = jnp.sum(
        jnp.where(diagonal, jnp.broadcast_to(rate, (rows, rows)), 0.0), axis=0, keepdims=True
    )


def summary_kernel(k_ref, *refs):
    for first in range(0, k_ref.shape[1], BLK):
        summary_block(first, k_ref, *refs)


VMEM_SPEC = pl.BlockSpec(memory_space=pltpu.VMEM)
ANY_SPEC = pl.BlockSpec(memory_space=pl.ANY)
PARAMS = pltpu.CompilerParams(vmem_limit_bytes=24 << 20)


def cost(flops, bytes_accessed):
    return pl.CostEstimate(flops=flops, bytes_accessed=bytes_accessed, transcendentals=0)


def summary_call(key_in, value, rates, residues):
    tokens, channels = key_in.shape
    modes = rates.shape[1]
    table = jax.ShapeDtypeStruct((channels // LANES * modes, LANES), F32)
    return pl.pallas_call(
        summary_kernel,
        in_specs=[VMEM_SPEC] * 4,
        out_specs=[VMEM_SPEC] * 4,
        out_shape=[table, table, table, jax.ShapeDtypeStruct((1, channels // GROUP * modes), F32)],
        compiler_params=PARAMS,
        cost_estimate=cost(2 * 3 * tokens * BLK * channels, 4 * tokens * channels),
        name="block_summary",
    )(key_in, value, rates, residues)


def local_kernel(
    chunk, modes, parts,
    k_ref, v_ref, rate_ref, residue_ref, skip_ref, state_ref, weight_ref,
    out_ref, end_ref, *rest,
):
    part_refs, (u_ref, sems) = rest[: len(parts)], rest[len(parts) :]
    tiles = k_ref.shape[1] // LANES
    rows = slice(chunk * CHUNK, (chunk + 1) * CHUNK)
    copies = []
    if parts:
        me = lax.axis_index("tp")
        width = part_refs[0].shape[1]
        for i, part in enumerate(parts):
            at = pl.multiple_of((me ^ part) * width, width)
            copies.append(
                pltpu.make_async_copy(weight_ref.at[:, pl.ds(at, width)], part_refs[i], sems.at[i])
            )
            copies[-1].start()
    for tile in range(tiles):
        lanes = slice(tile * LANES, (tile + 1) * LANES)
        u = (k_ref[rows, lanes].astype(F32) * v_ref[rows, lanes].astype(F32)).astype(BF16)
        u_ref[tile * CHUNK : (tile + 1) * CHUNK, :] = u.astype(F32)
    decay = [jnp.exp(-rate_ref[pl.ds(m, tiles, stride=modes), :]) for m in range(modes)]
    residue = [residue_ref[pl.ds(m, tiles, stride=modes), :] for m in range(modes)]
    skip = skip_ref[...]

    def step(t, states):
        u = u_ref[pl.ds(t, tiles, stride=CHUNK), :]
        states = tuple(d * s + u for d, s in zip(decay, states))
        terms = [skip * u] + [r * s for r, s in zip(residue, states)]
        while len(terms) > 1:
            terms = [a + b for a, b in zip(terms[::2], terms[1::2])] + (
                [terms[-1]] if len(terms) % 2 else []
            )
        out_ref[pl.ds(t, tiles, stride=CHUNK), :] = terms[0]
        return states

    first = tuple(state_ref[m * tiles : (m + 1) * tiles, :] for m in range(modes))
    last = lax.fori_loop(0, CHUNK, step, first, unroll=4)
    for m in range(modes):
        end_ref[m * tiles : (m + 1) * tiles, :] = last[m]
    for copy in copies:
        copy.wait()


def local_call(chunk, parts, key_in, value, rate_table, residue_table, skip_tiles, state, weight, width):
    channels = key_in.shape[1]
    tiles = channels // LANES
    modes = rate_table.shape[0] // tiles
    part_shape = jax.ShapeDtypeStruct((channels, width), weight.dtype)
    return pl.pallas_call(
        lambda *refs: local_kernel(chunk, modes, parts, *refs),
        in_specs=[VMEM_SPEC] * 6 + [ANY_SPEC],
        out_specs=[VMEM_SPEC] * 2 + [ANY_SPEC] * len(parts),
        out_shape=[
            jax.ShapeDtypeStruct((CHUNK * tiles, LANES), F32),
            jax.ShapeDtypeStruct((modes * tiles, LANES), F32),
        ]
        + [part_shape] * len(parts),
        scratch_shapes=[
            pltpu.VMEM((tiles * CHUNK, LANES), F32),
            pltpu.SemaphoreType.DMA((max(len(parts), 1),)),
        ],
        compiler_params=PARAMS,
        cost_estimate=cost(4 * modes * CHUNK * channels, 8 * CHUNK * channels),
        name="local_conv",
    )(key_in, value, rate_table, residue_table, skip_tiles, state, weight)


def mix_kernel(chunk, modes, q_ref, local_ref, state_ref, residue_ref, flat_ref, out_ref):
    groups = BLK // GROUP
    tiles = BLK // LANES
    rows = groups * modes
    tokens = slice(chunk * CHUNK, (chunk + 1) * CHUNK)
    mask = group_mask(groups, modes, BLK)
    since = lax.broadcasted_iota(jnp.int32, (CHUNK, rows), 0).astype(F32) + (chunk * CHUNK + 1.0)
    for block in range(q_ref.shape[1] // BLK):
        tile0 = block * tiles
        weighted = [
            state_ref[i * modes : (i + 1) * modes, :] * residue_ref[i * modes : (i + 1) * modes, :]
            for i in range(tile0, tile0 + tiles)
        ]
        spread = jnp.broadcast_to(jnp.concatenate(weighted, axis=1)[None], (groups, modes, BLK))
        spread = jnp.where(mask, spread, 0.0).reshape(rows, BLK)
        flat = flat_ref[:, block * rows : (block + 1) * rows]
        decay_hi, decay_lo = split_bf16(jnp.exp(-flat * since), 2)
        state_hi, state_lo = split_bf16(spread, 2)
        past = dot(decay_lo, state_hi) + dot(decay_hi, state_lo) + dot(decay_hi, state_hi)
        for tile in range(tiles):
            lanes = slice((tile0 + tile) * LANES, (tile0 + tile + 1) * LANES)
            conv = local_ref[(tile0 + tile) * CHUNK : (tile0 + tile + 1) * CHUNK, :]
            conv = conv + past[:, tile * LANES : (tile + 1) * LANES]
            out_ref[:, lanes] = (q_ref[tokens, lanes].astype(F32) * conv).astype(BF16)


def mix_call(chunk, query, local, state, residue_table, flat_rates):
    channels = query.shape[1]
    modes = flat_rates.shape[1] * GROUP // channels
    return pl.pallas_call(
        lambda *refs: mix_kernel(chunk, modes, *refs),
        in_specs=[VMEM_SPEC] * 5,
        out_specs=VMEM_SPEC,
        out_shape=jax.ShapeDtypeStruct((CHUNK, channels), BF16),
        compiler_params=PARAMS,
        cost_estimate=cost(2 * 3 * CHUNK * BLK * channels, 8 * CHUNK * channels),
        name="mix",
    )(query, local, state, residue_table, flat_rates)


def project_kernel(own_ref, pair_ref, own_w_ref, pair_w_ref, out_ref):
    cols = 256
    for at in range(0, out_ref.shape[1], cols):
        lanes = slice(at, at + cols)
        total = dot(own_ref[...], own_w_ref[:, lanes]) + dot(pair_ref[...], pair_w_ref[:, lanes])
        out_ref[:, lanes] = total.astype(out_ref.dtype)


def project_call(mixed, mixed_pair, weight, weight_pair, out_dtype):
    tokens, depth = mixed.shape
    width = weight.shape[1]
    return pl.pallas_call(
        project_kernel,
        in_specs=[VMEM_SPEC] * 4,
        out_specs=VMEM_SPEC,
        out_shape=jax.ShapeDtypeStruct((tokens, width), out_dtype),
        compiler_params=PARAMS,
        cost_estimate=cost(4 * tokens * depth * width, 4 * depth * width + 4 * tokens * width),
        name="project",
    )(mixed, mixed_pair, weight, weight_pair)


def add_kernel(near_ref, arrived_ref, *refs):
    refs[-1][...] = (near_ref[...] + arrived_ref[...].astype(F32)).astype(BF16)


def add_call(chunk, near, arrived, out, tokens):
    width = near.shape[1]
    block = pl.BlockSpec((CHUNK, width), lambda i: (0, 0))
    args = [near, arrived] + ([] if out is None else [out])
    return pl.pallas_call(
        add_kernel,
        grid=(1,),
        in_specs=[block, block] + [ANY_SPEC] * (len(args) - 2),
        out_specs=pl.BlockSpec((CHUNK, width), lambda i: (chunk, 0)),
        out_shape=jax.ShapeDtypeStruct((tokens, width), BF16),
        input_output_aliases={} if out is None else {2: 0},
        compiler_params=PARAMS,
        cost_estimate=cost(CHUNK * width, 8 * CHUNK * width),
        name="add_arrived",
    )(*args)


def tie(*arrays):
    return lax.optimization_barrier(arrays)


def shards(query, key_in, value, rates, residues, skip_gain, out_weight, *, n_ctx, n_tp):
    tokens, channels = query.shape
    width = out_weight.shape[1] // n_tp
    tiles = channels // LANES
    chunks = tokens // CHUNK
    block = lax.axis_index("ctx")

    def swap(x, bit):
        return lax.ppermute(x, "tp", [(i, i ^ bit) for i in range(n_tp)])

    total, rate_table, residue_table, flat_rates = summary_call(key_in, value, rates, residues)
    skip_tiles = skip_gain.reshape(tiles, LANES)
    carry = jnp.zeros((tiles * rates.shape[1], LANES), F32)
    out_weight = pltpu.with_memory_space_constraint(out_weight, pltpu.HBM)
    local, parts = [], []

    def next_local():
        chunk = len(local)
        wanted = {0: (2, 3), 1: (0, 1)}.get(chunk, ())
        out, end, *got = local_call(
            chunk, wanted, key_in, value, rate_table, residue_table, skip_tiles, carry, out_weight, width
        )
        local.append(out)
        parts.extend(got)
        return end

    def decayed(blocks):
        return jnp.exp(-rate_table * (blocks * tokens).astype(F32))

    state = jnp.zeros_like(total)
    span = 1
    while span < n_ctx:
        last = 2 * span >= n_ctx
        pairs = [(i, i ^ span) for i in range(n_ctx) if not (last and i & span)]
        other = lax.ppermute(total, "ctx", pairs)
        if len(local) < chunks:
            carry = next_local()
            if last:
                while len(local) < chunks:
                    carry = next_local()
            other, carry = tie(other, carry)
        upper = (block & span) != 0
        state = jnp.where(upper, state + decayed(block & (span - 1)) * other, state)
        over = decayed(jnp.int32(span))
        total = jnp.where(upper, total + over * other, other + over * total)
        if not last:
            total, carry = tie(total, carry)
        span *= 2
    while len(local) < chunks:
        carry = next_local()
    far, far_send, near, near_send = parts
    pair_far = swap(far_send, 1)
    pair_near = swap(near_send, 1)

    mixed = [mix_call(c, query, local[c], state, residue_table, flat_rates) for c in range(chunks)]
    mixed_pair = [swap(m, 1) for m in mixed]
    arrived = [
        swap(project_call(m, p, far, pair_far, BF16), 2) for m, p in zip(mixed, mixed_pair)
    ]
    out = None
    for c in range(chunks):
        here = project_call(mixed[c], mixed_pair[c], near, pair_near, F32)
        out = add_call(c, here, arrived[c], out, tokens)
    return out


def solution(mesh):
    n_ctx, n_tp = mesh.shape["ctx"], mesh.shape["tp"]
    in_specs = (
        P("ctx", "tp"),
        P("ctx", "tp"),
        P("ctx", "tp"),
        P("tp", None),
        P("tp", None),
        P("tp"),
        P("tp", None),
    )

    def body(*args):
        return shards(*args, n_ctx=n_ctx, n_tp=n_tp)

    return jax.shard_map(body, mesh=mesh, in_specs=in_specs, out_specs=P("ctx", "tp"), check_vma=False)
```

```python
import jax
import jax.numpy as jnp
from jax import lax
from jax.experimental import pallas as pl
from jax.experimental.pallas import tpu as pltpu
from jax.sharding import PartitionSpec as P

GROUP = 16
LANES = 128
BLK = 256
SEG = 256
CHUNK = 128
F32, BF16 = jnp.float32, jnp.bfloat16
VMEM_SPEC = pl.BlockSpec(memory_space=pltpu.VMEM)
HBM_SPEC = pl.BlockSpec(memory_space=pltpu.HBM)
ANY_SPEC = pl.BlockSpec(memory_space=pl.ANY)
PARAMS = pltpu.CompilerParams(vmem_limit_bytes=16 << 20)


COST = pl.CostEstimate(flops=1, bytes_accessed=1, transcendentals=0)


def in_hbm(x):
    return pltpu.with_memory_space_constraint(x, pltpu.HBM)


def shape(dims, dtype=F32):
    return jax.ShapeDtypeStruct(dims, dtype)


def split_bf16(x, parts):
    pieces = []
    for _ in range(parts):
        piece = x.astype(BF16)
        pieces.append(piece)
        x = x - piece.astype(F32)
    return pieces


def dot(a, b):
    return lax.dot_general(a, b, (((1,), (0,)), ((), ())), preferred_element_type=F32)


def group_mask(groups, modes, channels):
    dims = (groups, modes, channels)
    return lax.broadcasted_iota(jnp.int32, dims, 0) == (
        lax.broadcasted_iota(jnp.int32, dims, 2) // GROUP
    )


def column_of(table, first, groups):
    modes, width = table.shape
    rows = groups * modes
    spread = jnp.broadcast_to(table[None], (groups, modes, width)).reshape(rows, width)
    pick = lax.broadcasted_iota(jnp.int32, (rows, width), 1) == (
        lax.broadcasted_iota(jnp.int32, (rows, width), 0) // modes + first
    )
    return jnp.sum(jnp.where(pick, spread, 0.0), axis=1, keepdims=True)


def summary_kernel(
    k_hbm, v_hbm, rates_ref, residues_ref,
    sum_ref, rate_ref, residue_ref, flat_ref, u_ref,
    k_ref, v_ref, sems,
):
    tokens, channels = u_ref.shape
    modes = rates_ref.shape[0]
    groups = BLK // GROUP
    rows = groups * modes
    blocks = channels // BLK
    copies = []
    for block in range(blocks):
        lanes = pl.ds(block * BLK, BLK)
        for i, (src, dst) in enumerate(((k_hbm, k_ref), (v_hbm, v_ref))):
            copies.append(
                pltpu.make_async_copy(src.at[:, lanes], dst.at[:, lanes], sems.at[2 * block + i])
            )
            copies[-1].start()
    mask = group_mask(groups, modes, BLK)
    position = lax.broadcasted_iota(jnp.int32, (rows, SEG), 1).astype(F32)
    diagonal = lax.broadcasted_iota(jnp.int32, (rows, rows), 0) == lax.broadcasted_iota(
        jnp.int32, (rows, rows), 1
    )

    def store(ref, block, dense):
        kept = jnp.where(mask, dense.reshape(groups, modes, BLK), 0.0)
        table = jnp.sum(kept, axis=0)
        for tile in range(BLK // LANES):
            at = (block * (BLK // LANES) + tile) * modes
            ref[at : at + modes, :] = table[:, tile * LANES : (tile + 1) * LANES]

    for block in range(blocks):
        lanes = slice(block * BLK, (block + 1) * BLK)
        rate = column_of(rates_ref[...], block * groups, groups)
        residue = column_of(residues_ref[...], block * groups, groups)
        decay = split_bf16(jnp.exp(-rate * (SEG - 1.0 - position)), 3)
        carry = jnp.exp(-rate * float(SEG))
        store(rate_ref, block, jnp.broadcast_to(rate, (rows, BLK)))
        store(residue_ref, block, jnp.broadcast_to(residue, (rows, BLK)))
        flat_ref[:, block * rows : (block + 1) * rows] = jnp.sum(
            jnp.where(diagonal, jnp.broadcast_to(rate, (rows, rows)), 0.0), axis=0, keepdims=True
        )
        for copy in copies[2 * block : 2 * block + 2]:
            copy.wait()
        dense = None
        for at in range(0, tokens, SEG):
            part = slice(at, at + SEG)
            u = (k_ref[part, lanes].astype(F32) * v_ref[part, lanes].astype(F32)).astype(BF16)
            u_ref[part, lanes] = u
            here = dot(decay[2], u) + dot(decay[1], u) + dot(decay[0], u)
            dense = here if dense is None else dense * carry + here
        store(sum_ref, block, dense)


def summary_call(key_in, value, rates_t, residues_t):
    tokens, channels = key_in.shape
    modes = rates_t.shape[0]
    table = shape((channels // LANES * modes, LANES))
    return pl.pallas_call(
        summary_kernel,
        in_specs=[HBM_SPEC] * 2 + [VMEM_SPEC] * 2,
        out_specs=[VMEM_SPEC] * 5,
        out_shape=[
            table, table, table,
            shape((1, channels // GROUP * modes)),
            shape((tokens, channels), BF16),
        ],
        scratch_shapes=[
            pltpu.VMEM((tokens, channels), BF16),
            pltpu.VMEM((tokens, channels), BF16),
            pltpu.SemaphoreType.DMA((2 * channels // BLK,)),
        ],
        compiler_params=PARAMS,
        cost_estimate=COST,
        name="block_summary",
    )(in_hbm(key_in), in_hbm(value), rates_t, residues_t)


def local_kernel(
    chunk, modes, parts, started,
    u_in, rate_ref, residue_ref, skip_ref, q_hbm, weight_hbm, after_ref, *rest,
):
    carry_ref = rest[0] if started else None
    out_ref, end_ref, q_ref, *rest = rest[started:]
    u_ref, sems = rest[-2:]
    tiles = u_in.shape[1] // LANES
    rows = slice(chunk * CHUNK, (chunk + 1) * CHUNK)
    copies = [pltpu.make_async_copy(q_hbm.at[pl.ds(chunk * CHUNK, CHUNK), :], q_ref, sems.at[0])]
    if parts:
        me = lax.axis_index("tp")
        parts_ref = rest[0]
        depth, width = weight_hbm.shape[0], parts_ref.shape[1]
        for i, part in enumerate(parts):
            src = weight_hbm.at[:, pl.ds(pl.multiple_of((me ^ part) * width, width), width)]
            dst = parts_ref.at[pl.ds(i * depth, depth), :]
            copies.append(pltpu.make_async_copy(src, dst, sems.at[i + 1]))
    for copy in copies:
        copy.start()
    for tile in range(tiles):
        u = u_in[rows, tile * LANES : (tile + 1) * LANES]
        u_ref[tile * CHUNK : (tile + 1) * CHUNK, :] = u.astype(F32)
    decay = [jnp.exp(-rate_ref[pl.ds(m, tiles, stride=modes), :]) for m in range(modes)]
    residue = [residue_ref[pl.ds(m, tiles, stride=modes), :] for m in range(modes)]
    skip = skip_ref[...]

    def step(t, states):
        u = u_ref[pl.ds(t, tiles, stride=CHUNK), :]
        states = tuple(d * s + u for d, s in zip(decay, states))
        terms = [skip * u] + [r * s for r, s in zip(residue, states)]
        while len(terms) > 1:
            terms = [a + b for a, b in zip(terms[::2], terms[1::2])] + (
                [terms[-1]] if len(terms) % 2 else []
            )
        out_ref[pl.ds(t, tiles, stride=CHUNK), :] = terms[0]
        return states

    if started:
        first = tuple(carry_ref[m * tiles : (m + 1) * tiles, :] for m in range(modes))
    else:
        first = (jnp.zeros((tiles, LANES), F32),) * modes
    last = lax.fori_loop(0, CHUNK, step, first, unroll=4)
    for m in range(modes):
        end_ref[m * tiles : (m + 1) * tiles, :] = last[m]
    for copy in copies:
        copy.wait()


def local_call(chunk, parts, u, rate_table, residue_table, skip_tiles, query, weight, after, carry, width):
    channels = u.shape[1]
    tiles = channels // LANES
    modes = rate_table.shape[0] // tiles
    started = carry is not None
    return pl.pallas_call(
        lambda *refs: local_kernel(chunk, modes, parts, started, *refs),
        in_specs=[VMEM_SPEC] * 4 + [HBM_SPEC] * 2 + [ANY_SPEC] + [VMEM_SPEC] * started,
        out_specs=[VMEM_SPEC] * (3 + bool(parts)),
        out_shape=[
            shape((CHUNK * tiles, LANES)),
            shape((modes * tiles, LANES)),
            shape((CHUNK, channels), BF16),
        ]
        + [shape((len(parts) * channels, width), BF16)] * bool(parts),
        scratch_shapes=[
            pltpu.VMEM((tiles * CHUNK, LANES), F32),
            pltpu.SemaphoreType.DMA((1 + len(parts),)),
        ],
        compiler_params=PARAMS,
        cost_estimate=COST,
        name="local_conv",
    )(
        u, rate_table, residue_table, skip_tiles, in_hbm(query), in_hbm(weight), after,
        *([carry] if started else []),
    )


def double(span, tokens, rate, total, state, other):
    block = lax.axis_index("ctx")
    upper = (block & span) != 0
    before = ((block & (span - 1)) * tokens).astype(F32)
    state = jnp.where(upper, state + jnp.exp(-rate * before) * other, state)
    over = jnp.exp(-rate * float(span * tokens))
    total = jnp.where(upper, total + over * other, other + over * total)
    return total, state


def join_kernel(span, tokens, passed_ref, rate_ref, other_ref, total_ref, *refs):
    state = refs[0][...] if len(refs) == 4 else jnp.zeros(rate_ref.shape, F32)
    refs[-2][...], refs[-1][...] = double(
        span, tokens, rate_ref[...], total_ref[...], state, other_ref[...]
    )


def join_call(span, tokens, passed, rate_table, other, total, state):
    args = [passed, rate_table, other, total] + ([] if state is None else [state])
    return pl.pallas_call(
        lambda *refs: join_kernel(span, tokens, *refs),
        in_specs=[ANY_SPEC] + [VMEM_SPEC] * (len(args) - 1),
        out_specs=[ANY_SPEC] + [VMEM_SPEC] * 2,
        out_shape=[shape(passed.shape, passed.dtype)] + [shape(total.shape)] * 2,
        input_output_aliases={0: 0},
        compiler_params=PARAMS,
        cost_estimate=COST,
        name="join_blocks",
    )(*args)


def mix_kernel(chunk, modes, q_ref, local_ref, residue_ref, flat_ref, state_ref, after_ref, out_ref):
    groups = BLK // GROUP
    tiles = BLK // LANES
    rows = groups * modes
    mask = group_mask(groups, modes, BLK)
    since = lax.broadcasted_iota(jnp.int32, (CHUNK, rows), 0).astype(F32) + (chunk * CHUNK + 1.0)
    for block in range(q_ref.shape[1] // BLK):
        tile0 = block * tiles
        weighted = [
            state_ref[i * modes : (i + 1) * modes, :] * residue_ref[i * modes : (i + 1) * modes, :]
            for i in range(tile0, tile0 + tiles)
        ]
        spread = jnp.broadcast_to(jnp.concatenate(weighted, axis=1)[None], (groups, modes, BLK))
        spread = jnp.where(mask, spread, 0.0).reshape(rows, BLK)
        flat = flat_ref[:, block * rows : (block + 1) * rows]
        decay_hi, decay_lo = split_bf16(jnp.exp(-flat * since), 2)
        state_hi, state_lo = split_bf16(spread, 2)
        past = dot(decay_lo, state_hi) + dot(decay_hi, state_lo) + dot(decay_hi, state_hi)
        for tile in range(tiles):
            lanes = slice((tile0 + tile) * LANES, (tile0 + tile + 1) * LANES)
            conv = local_ref[(tile0 + tile) * CHUNK : (tile0 + tile + 1) * CHUNK, :]
            conv = conv + past[:, tile * LANES : (tile + 1) * LANES]
            out_ref[:, lanes] = (q_ref[:, lanes].astype(F32) * conv).astype(BF16)


def mix_call(chunk, query, local, residue_table, flat_rates, state, after):
    channels = query.shape[1]
    modes = flat_rates.shape[1] * GROUP // channels
    return pl.pallas_call(
        lambda *refs: mix_kernel(chunk, modes, *refs),
        in_specs=[VMEM_SPEC] * 5 + [ANY_SPEC],
        out_specs=VMEM_SPEC,
        out_shape=shape((CHUNK, channels), BF16),
        compiler_params=PARAMS,
        cost_estimate=COST,
        name="mix",
    )(query, local, residue_table, flat_rates, state, after)


def project_kernel(row, first, count, own_w_ref, pair_w_ref, *refs):
    cols = 256
    own_refs, pair_refs, out_ref = refs[:count], refs[count : 2 * count], refs[-1]
    rows_w = slice(row, row + own_refs[0].shape[1])
    for at in range(0, out_ref.shape[1], cols):
        lanes = slice(first + at, first + at + cols)
        for i, (own, pair) in enumerate(zip(own_refs, pair_refs)):
            total = dot(own[...], own_w_ref[rows_w, lanes]) + dot(pair[...], pair_w_ref[rows_w, lanes])
            rows = slice(i * CHUNK, (i + 1) * CHUNK)
            out_ref[rows, at : at + cols] = total.astype(out_ref.dtype)


def project_call(row, first, width, mixed, mixed_pair, weight, weight_pair, after, out_dtype):
    count = len(mixed)
    return pl.pallas_call(
        lambda *refs: project_kernel(row, first, count, *refs),
        in_specs=[VMEM_SPEC] * (2 + 2 * count) + [ANY_SPEC] * len(after),
        out_specs=VMEM_SPEC,
        out_shape=shape((CHUNK * count, width), out_dtype),
        compiler_params=PARAMS,
        cost_estimate=COST,
        name="project",
    )(weight, weight_pair, *mixed, *mixed_pair, *after)


def add_kernel(near_ref, *refs):
    out_ref = refs[-1]
    at = 0
    for ref in refs[:-1]:
        if ref.dtype == BF16 and ref.shape[0] == CHUNK:
            lanes = slice(at, at + ref.shape[1])
            out_ref[:, lanes] = (near_ref[:, lanes] + ref[...].astype(F32)).astype(BF16)
            at += ref.shape[1]


def add_call(chunk, near, arrived, out):
    tokens, width = near.shape
    args = [near, *arrived] + ([] if out is None else [out])
    row = lambda i: (chunk, 0)
    return pl.pallas_call(
        add_kernel,
        grid=(1,),
        in_specs=[pl.BlockSpec((CHUNK, width), row)]
        + [pl.BlockSpec(a.shape, lambda i: (0, 0)) for a in arrived]
        + [ANY_SPEC] * (out is not None),
        out_specs=pl.BlockSpec((CHUNK, width), row),
        out_shape=shape((tokens, width), BF16),
        input_output_aliases={} if out is None else {len(args) - 1: 0},
        compiler_params=PARAMS,
        cost_estimate=COST,
        name="add_arrived",
    )(*args)


def shards(query, key_in, value, rates, residues, skip_gain, out_weight, *, n_ctx, n_tp):
    tokens, channels = query.shape
    width = out_weight.shape[1] // n_tp
    chunks = tokens // CHUNK

    def swap(x, bit):
        return lax.ppermute(x, "tp", [(i, i ^ bit) for i in range(n_tp)])

    total, rate_table, residue_table, flat_rates, u = summary_call(
        key_in, value, rates.T, residues.T
    )
    skip_tiles = skip_gain.reshape(channels // LANES, LANES)
    local, q, parts = [], [], []

    def next_local(after, carry):
        chunk = len(local)
        wanted = {0: (3, 1), 1: (2, 0)}.get(chunk, ())
        out, carry, q_rows, *got = local_call(
            chunk, wanted, u, rate_table, residue_table, skip_tiles, query, out_weight, after, carry, width
        )
        local.append(out)
        q.append(q_rows)
        parts.extend(got)
        return carry

    state = carry = weight_pair = None
    span = 1
    while span < n_ctx:
        last = 2 * span >= n_ctx
        pairs = [(i, i ^ span) for i in range(n_ctx) if not (last and i & span)]
        other = lax.ppermute(total, "ctx", pairs)
        while len(local) < chunks:
            carry = next_local(total, carry)
            if not last:
                break
        passed = parts[0] if span == 1 else carry
        passed, total, state = join_call(span, tokens, passed, rate_table, other, total, state)
        if span == 1:
            weight_pair = swap(passed, 1)
        else:
            carry = passed
        span *= 2
    weight = parts[1]

    mixed, mixed_pair, after = [], [], carry
    for c in range(chunks):
        after = mix_call(c, q[c], local[c], residue_table, flat_rates, state, after)
        mixed.append(after)
        mixed_pair.append(swap(after, 1))
    arrived = []
    for c in range(chunks):
        pieces = 2 if c == 0 else 1
        arrived.append([])
        earlier = arrived[0] if c == chunks - 1 else []
        for piece in range(pieces):
            cols = width // pieces
            after = project_call(
                0, piece * cols, cols, mixed[c : c + 1], mixed_pair[c : c + 1], weight, weight_pair, [after, *earlier], BF16
            )
            arrived[c].append(swap(after, 2))
    here = project_call(channels, 0, width, mixed, mixed_pair, weight, weight_pair, [after], F32)
    out = None
    for c in range(chunks):
        out = add_call(c, here, arrived[c], out)
    return out


def solution(mesh):
    n_ctx, n_tp = mesh.shape["ctx"], mesh.shape["tp"]
    in_specs = (
        P("ctx", "tp"),
        P("ctx", "tp"),
        P("ctx", "tp"),
        P("tp", None),
        P("tp", None),
        P("tp"),
        P("tp", None),
    )

    def body(*args):
        return shards(*args, n_ctx=n_ctx, n_tp=n_tp)

    return jax.shard_map(body, mesh=mesh, in_specs=in_specs, out_specs=P("ctx", "tp"), check_vma=False)
```

```python
import jax
import jax.numpy as jnp
from jax import lax
from jax.experimental import pallas as pl
from jax.experimental.pallas import tpu as pltpu
from jax.sharding import PartitionSpec as P

GROUP = 16
LANES = 128
BLK = 256
SEG = 256
CHUNK = 128
F32, BF16 = jnp.float32, jnp.bfloat16
VMEM_SPEC = pl.BlockSpec(memory_space=pltpu.VMEM)
HBM_SPEC = pl.BlockSpec(memory_space=pltpu.HBM)
ANY_SPEC = pl.BlockSpec(memory_space=pl.ANY)
PARAMS = pltpu.CompilerParams(vmem_limit_bytes=16 << 20)


COST = pl.CostEstimate(flops=1, bytes_accessed=1, transcendentals=0)


def in_hbm(x):
    return pltpu.with_memory_space_constraint(x, pltpu.HBM)


def shape(dims, dtype=F32):
    return jax.ShapeDtypeStruct(dims, dtype)


def split_bf16(x, parts):
    pieces = []
    for _ in range(parts):
        piece = x.astype(BF16)
        pieces.append(piece)
        x = x - piece.astype(F32)
    return pieces


def dot(a, b):
    return lax.dot_general(a, b, (((1,), (0,)), ((), ())), preferred_element_type=F32)


def group_mask(groups, modes, channels):
    dims = (groups, modes, channels)
    return lax.broadcasted_iota(jnp.int32, dims, 0) == (
        lax.broadcasted_iota(jnp.int32, dims, 2) // GROUP
    )


def column_of(table, first, groups):
    modes, width = table.shape
    rows = groups * modes
    spread = jnp.broadcast_to(table[None], (groups, modes, width)).reshape(rows, width)
    pick = lax.broadcasted_iota(jnp.int32, (rows, width), 1) == (
        lax.broadcasted_iota(jnp.int32, (rows, width), 0) // modes + first
    )
    return jnp.sum(jnp.where(pick, spread, 0.0), axis=1, keepdims=True)


def summary_kernel(
    k_hbm, v_hbm, rates_hbm, residues_hbm, skip_hbm,
    sum_ref, rate_ref, residue_ref, flat_ref, u_ref, skip_ref,
    k_ref, v_ref, rates_ref, residues_ref, decay_ref, sems,
):
    tokens, channels = u_ref.shape
    modes = rates_ref.shape[0]
    groups = BLK // GROUP
    rows = groups * modes
    blocks = channels // BLK
    tiles = BLK // LANES
    segments = tokens // SEG
    small = [
        pltpu.make_async_copy(src, dst, sems.at[i])
        for i, (src, dst) in enumerate(
            ((rates_hbm, rates_ref), (residues_hbm, residues_ref), (skip_hbm, skip_ref))
        )
    ]
    large = []
    for seg in range(segments):
        part = pl.ds(seg * SEG, SEG)
        for i, (src, dst) in enumerate(((k_hbm, k_ref), (v_hbm, v_ref))):
            sem = sems.at[len(small) + 2 * seg + i]
            large.append(pltpu.make_async_copy(src.at[part, :], dst.at[part, :], sem))
    for copy in small + large:
        copy.start()
    for copy in small:
        copy.wait()
    mask = group_mask(groups, modes, BLK)
    position = lax.broadcasted_iota(jnp.int32, (rows, SEG), 1).astype(F32)
    diagonal = lax.broadcasted_iota(jnp.int32, (rows, rows), 0) == lax.broadcasted_iota(
        jnp.int32, (rows, rows), 1
    )

    def compact(dense):
        return jnp.sum(jnp.where(mask, dense.reshape(groups, modes, BLK), 0.0), axis=0)

    def tile_rows(block, tile):
        at = (block * tiles + tile) * modes
        return slice(at, at + modes), slice(tile * LANES, (tile + 1) * LANES)

    for block in range(blocks):
        rate = column_of(rates_ref[...], block * groups, groups)
        residue = column_of(residues_ref[...], block * groups, groups)
        hi, lo = split_bf16(jnp.exp(-rate * (SEG - 1.0 - position)), 2)
        decay_ref[2 * block * rows : (2 * block + 1) * rows, :] = hi
        decay_ref[(2 * block + 1) * rows : (2 * block + 2) * rows, :] = lo
        flat_ref[:, block * rows : (block + 1) * rows] = jnp.sum(
            jnp.where(diagonal, jnp.broadcast_to(rate, (rows, rows)), 0.0), axis=0, keepdims=True
        )
        for ref, column in ((rate_ref, rate), (residue_ref, residue)):
            table = compact(jnp.broadcast_to(column, (rows, BLK)))
            for tile in range(tiles):
                at, lanes = tile_rows(block, tile)
                ref[at, :] = table[:, lanes]
    for seg in range(segments):
        part = slice(seg * SEG, (seg + 1) * SEG)
        for copy in large[2 * seg : 2 * seg + 2]:
            copy.wait()
        for block in range(blocks):
            lanes = slice(block * BLK, (block + 1) * BLK)
            u = (k_ref[part, lanes].astype(F32) * v_ref[part, lanes].astype(F32)).astype(BF16)
            u_ref[part, lanes] = u
            both = dot(decay_ref[2 * block * rows : (2 * block + 2) * rows, :], u)
            here = compact(both[:rows] + both[rows:])
            for tile in range(tiles):
                at, lanes = tile_rows(block, tile)
                part_sum = here[:, lanes]
                if seg:
                    part_sum = part_sum + jnp.exp(-rate_ref[at, :] * float(SEG)) * sum_ref[at, :]
                sum_ref[at, :] = part_sum


def summary_call(key_in, value, rates_t, residues_t, skip_tiles):
    tokens, channels = key_in.shape
    modes = rates_t.shape[0]
    table = shape((channels // LANES * modes, LANES))
    return pl.pallas_call(
        summary_kernel,
        in_specs=[HBM_SPEC] * 5,
        out_specs=[VMEM_SPEC] * 6,
        out_shape=[
            table, table, table,
            shape((1, channels // GROUP * modes)),
            shape((tokens, channels), BF16),
            shape(skip_tiles.shape),
        ],
        scratch_shapes=[
            pltpu.VMEM((tokens, channels), BF16),
            pltpu.VMEM((tokens, channels), BF16),
            pltpu.VMEM(rates_t.shape, F32),
            pltpu.VMEM(rates_t.shape, F32),
            pltpu.VMEM((2 * channels // GROUP * modes, SEG), BF16),
            pltpu.SemaphoreType.DMA((3 + 2 * tokens // SEG,)),
        ],
        compiler_params=PARAMS,
        cost_estimate=COST,
        name="block_summary",
    )(*[in_hbm(x) for x in (key_in, value, rates_t, residues_t, skip_tiles)])


def local_kernel(
    begin, count, modes, parts, started,
    u_in, rate_ref, residue_ref, skip_ref, q_hbm, weight_hbm, *rest,
):
    carry_ref = rest[1] if started else None
    out_ref, end_ref, q_ref, *rest = rest[1 + started :]
    u_ref, sems = rest[-2:]
    tiles = u_in.shape[1] // LANES
    rows = slice(begin, begin + count)
    copies = [pltpu.make_async_copy(q_hbm.at[pl.ds(begin, count), :], q_ref, sems.at[0])]
    if parts:
        me = lax.axis_index("tp")
        parts_ref = rest[0]
        depth, width = weight_hbm.shape[0], parts_ref.shape[1]
        for i, part in enumerate(parts):
            src = weight_hbm.at[:, pl.ds(pl.multiple_of((me ^ part) * width, width), width)]
            dst = parts_ref.at[pl.ds(i * depth, depth), :]
            copies.append(pltpu.make_async_copy(src, dst, sems.at[i + 1]))
    for copy in copies:
        copy.start()
    for tile in range(tiles):
        u = u_in[rows, tile * LANES : (tile + 1) * LANES]
        u_ref[tile * count : (tile + 1) * count, :] = u.astype(F32)
    decay = [jnp.exp(-rate_ref[pl.ds(m, tiles, stride=modes), :]) for m in range(modes)]
    residue = [residue_ref[pl.ds(m, tiles, stride=modes), :] for m in range(modes)]
    skip = skip_ref[...]

    def step(t, states):
        u = u_ref[pl.ds(t, tiles, stride=count), :]
        states = tuple(d * s + u for d, s in zip(decay, states))
        terms = [skip * u] + [r * s for r, s in zip(residue, states)]
        while len(terms) > 1:
            terms = [a + b for a, b in zip(terms[::2], terms[1::2])] + (
                [terms[-1]] if len(terms) % 2 else []
            )
        out_ref[pl.ds(t, tiles, stride=count), :] = terms[0]
        return states

    if started:
        first = tuple(carry_ref[m * tiles : (m + 1) * tiles, :] for m in range(modes))
    else:
        first = (jnp.zeros((tiles, LANES), F32),) * modes
    last = lax.fori_loop(0, count, step, first, unroll=4)
    for m in range(modes):
        end_ref[m * tiles : (m + 1) * tiles, :] = last[m]
    for copy in copies:
        copy.wait()


def local_call(
    begin, count, parts, u, rate_table, residue_table, skip_tiles, query, weight, after, carry, width
):
    channels = u.shape[1]
    tiles = channels // LANES
    modes = rate_table.shape[0] // tiles
    started = carry is not None
    return pl.pallas_call(
        lambda *refs: local_kernel(begin, count, modes, parts, started, *refs),
        in_specs=[VMEM_SPEC] * 4 + [HBM_SPEC] * 2 + [ANY_SPEC] + [VMEM_SPEC] * started,
        out_specs=[VMEM_SPEC] * (3 + bool(parts)),
        out_shape=[
            shape((count * tiles, LANES)),
            shape((modes * tiles, LANES)),
            shape((count, channels), BF16),
        ]
        + [shape((len(parts) * channels, width), BF16)] * bool(parts),
        scratch_shapes=[
            pltpu.VMEM((tiles * count, LANES), F32),
            pltpu.SemaphoreType.DMA((1 + len(parts),)),
        ],
        compiler_params=PARAMS,
        cost_estimate=COST,
        name="local_conv",
    )(
        u, rate_table, residue_table, skip_tiles, in_hbm(query), in_hbm(weight), after,
        *([carry] if started else []),
    )


def double(span, tokens, rate, total, state, other):
    block = lax.axis_index("ctx")
    upper = (block & span) != 0
    before = ((block & (span - 1)) * tokens).astype(F32)
    state = jnp.where(upper, state + jnp.exp(-rate * before) * other, state)
    over = jnp.exp(-rate * float(span * tokens))
    total = jnp.where(upper, total + over * other, other + over * total)
    return total, state


def join_kernel(span, tokens, started, last, passed_ref, rate_ref, other_ref, total_ref, *refs):
    state = refs[0][...] if started else jnp.zeros(rate_ref.shape, F32)
    total, state = double(span, tokens, rate_ref[...], total_ref[...], state, other_ref[...])
    refs[-1][...] = state
    if not last:
        refs[-2][...] = total


def join_call(span, tokens, last, passed, rate_table, other, total, state):
    started = state is not None
    return pl.pallas_call(
        lambda *refs: join_kernel(span, tokens, started, last, *refs),
        in_specs=[ANY_SPEC] + [VMEM_SPEC] * (3 + started),
        out_specs=[ANY_SPEC] + [VMEM_SPEC] * (1 + (not last)),
        out_shape=[shape(passed.shape, passed.dtype)] + [shape(total.shape)] * (1 + (not last)),
        input_output_aliases={0: 0},
        compiler_params=PARAMS,
        cost_estimate=COST,
        name="join_blocks",
    )(passed, rate_table, other, total, *([state] if started else []))


def mix_kernel(begin, modes, outs, residue_ref, flat_ref, state_ref, after_ref, *refs):
    pieces, out_refs = list(zip(refs[:-outs:2], refs[1:-outs:2])), refs[-outs:]
    groups = BLK // GROUP
    tiles = BLK // LANES
    rows = groups * modes
    tokens = sum(ref.shape[0] for ref in out_refs)
    mask = group_mask(groups, modes, BLK)
    since = lax.broadcasted_iota(jnp.int32, (tokens, rows), 0).astype(F32) + (begin + 1.0)
    for block in range(out_refs[0].shape[1] // BLK):
        tile0 = block * tiles
        weighted = [
            state_ref[i * modes : (i + 1) * modes, :] * residue_ref[i * modes : (i + 1) * modes, :]
            for i in range(tile0, tile0 + tiles)
        ]
        spread = jnp.broadcast_to(jnp.concatenate(weighted, axis=1)[None], (groups, modes, BLK))
        spread = jnp.where(mask, spread, 0.0).reshape(rows, BLK)
        flat = flat_ref[:, block * rows : (block + 1) * rows]
        decay_hi, decay_lo = split_bf16(jnp.exp(-flat * since), 2)
        state_hi, state_lo = split_bf16(spread, 2)
        past = dot(decay_lo, state_hi) + dot(decay_hi, state_lo) + dot(decay_hi, state_hi)
        at = 0
        for q_ref, local_ref in pieces:
            count = q_ref.shape[0]
            for tile in range(tiles):
                lanes = slice((tile0 + tile) * LANES, (tile0 + tile + 1) * LANES)
                conv = local_ref[(tile0 + tile) * count : (tile0 + tile + 1) * count, :]
                conv = conv + past[at : at + count, tile * LANES : (tile + 1) * LANES]
                mixed = (q_ref[:, lanes].astype(F32) * conv).astype(BF16)
                first = 0
                for out_ref in out_refs:
                    last = first + out_ref.shape[0]
                    lo, hi = max(first, at), min(last, at + count)
                    if lo < hi:
                        out_ref[lo - first : hi - first, lanes] = mixed[lo - at : hi - at]
                    first = last
            at += count


def mix_call(begin, sizes, query, local, residue_table, flat_rates, state, after):
    channels = query[0].shape[1]
    modes = flat_rates.shape[1] * GROUP // channels
    pieces = [x for pair in zip(query, local) for x in pair]
    return pl.pallas_call(
        lambda *refs: mix_kernel(begin, modes, len(sizes), *refs),
        in_specs=[VMEM_SPEC] * 3 + [ANY_SPEC] + [VMEM_SPEC] * len(pieces),
        out_specs=[VMEM_SPEC] * len(sizes),
        out_shape=[shape((size, channels), BF16) for size in sizes],
        compiler_params=PARAMS,
        cost_estimate=COST,
        name="mix",
    )(residue_table, flat_rates, state, after, *pieces)


def project_kernel(row, pieces, own_w_ref, pair_w_ref, *refs):
    cols = 256
    count = len(pieces)
    own_refs, pair_refs, out_ref = refs[:count], refs[count : 2 * count], refs[-1]
    rows_w = slice(row, row + own_refs[0].shape[1])
    for first in range(0, out_ref.shape[1], cols):
        lanes = slice(first, first + cols)
        at = 0
        for own, pair, (begin, tokens) in zip(own_refs, pair_refs, pieces):
            rows = slice(begin, begin + tokens)
            total = dot(own[rows, :], own_w_ref[rows_w, lanes])
            total = total + dot(pair[rows, :], pair_w_ref[rows_w, lanes])
            out_ref[at : at + tokens, lanes] = total.astype(out_ref.dtype)
            at += tokens


def project_call(row, pieces, mixed, mixed_pair, weight, weight_pair, after, out_dtype):
    return pl.pallas_call(
        lambda *refs: project_kernel(row, pieces, *refs),
        in_specs=[VMEM_SPEC] * (2 + 2 * len(mixed)) + [ANY_SPEC] * len(after),
        out_specs=VMEM_SPEC,
        out_shape=shape((sum(tokens for _, tokens in pieces), weight.shape[1]), out_dtype),
        compiler_params=PARAMS,
        cost_estimate=COST,
        name="project",
    )(weight, weight_pair, *mixed, *mixed_pair, *after)


def add_kernel(near_ref, *refs):
    out_ref = refs[-1]
    at = 0
    for ref in refs[:-1]:
        if ref.dtype == BF16 and ref.shape[0] == CHUNK:
            lanes = slice(at, at + ref.shape[1])
            out_ref[:, lanes] = (near_ref[:, lanes] + ref[...].astype(F32)).astype(BF16)
            at += ref.shape[1]


def add_call(chunk, near, arrived, out):
    tokens, width = near.shape
    args = [near, *arrived] + ([] if out is None else [out])
    row = lambda i: (chunk, 0)
    return pl.pallas_call(
        add_kernel,
        grid=(1,),
        in_specs=[pl.BlockSpec((CHUNK, width), row)]
        + [pl.BlockSpec(a.shape, lambda i: (0, 0)) for a in arrived]
        + [ANY_SPEC] * (out is not None),
        out_specs=pl.BlockSpec((CHUNK, width), row),
        out_shape=shape((tokens, width), BF16),
        input_output_aliases={} if out is None else {len(args) - 1: 0},
        compiler_params=PARAMS,
        cost_estimate=COST,
        name="add_arrived",
    )(*args)


def shards(query, key_in, value, rates, residues, skip_gain, out_weight, *, n_ctx, n_tp):
    tokens, channels = query.shape
    width = out_weight.shape[1] // n_tp
    chunks = tokens // CHUNK

    def swap(x, bit):
        return lax.ppermute(x, "tp", [(i, i ^ bit) for i in range(n_tp)])

    skip_tiles = skip_gain.reshape(channels // LANES, LANES)
    total, rate_table, residue_table, flat_rates, u, skip_tiles = summary_call(
        key_in, value, rates.T, residues.T, skip_tiles
    )
    sizes = [CHUNK] + [(tokens - CHUNK) // 2] * 2
    local, q, parts = [], [], []

    def next_local(after, carry):
        index = len(local)
        wanted = {0: (3, 1), 1: (2, 0)}.get(index, ())
        out, carry, q_rows, *got = local_call(
            sum(sizes[:index]), sizes[index], wanted, u, rate_table, residue_table, skip_tiles,
            query, out_weight, after, carry, width,
        )
        local.append(out)
        q.append(q_rows)
        parts.extend(got)
        return carry

    state = carry = weight_pair = None
    span = 1
    while span < n_ctx:
        other = lax.ppermute(total, "ctx", [(i, i ^ span) for i in range(n_ctx)])
        if len(local) < len(sizes):
            carry = next_local(total, carry)
        last = 2 * span >= n_ctx
        passed = parts[0] if span == 1 else carry
        passed, *ends, state = join_call(span, tokens, last, passed, rate_table, other, total, state)
        if span == 1:
            weight_pair = swap(passed, 1)
        else:
            carry = passed
        if not last:
            total = ends[0]
        span *= 2
    while len(local) < len(sizes):
        carry = next_local(carry, carry)
    weight = parts[1]

    mixed = mix_call(0, [CHUNK], q[:1], local[:1], residue_table, flat_rates, state, carry)
    mixed += mix_call(
        CHUNK, [CHUNK] * (chunks - 1), q[1:], local[1:], residue_table, flat_rates, state, mixed[0]
    )
    other = [swap(x, 1) for x in mixed]
    arrived = []
    after = mixed[-1]
    for c in range(chunks):
        waits = [after] + (arrived[:1] if c == chunks - 1 else [])
        after = project_call(0, [(0, CHUNK)], [mixed[c]], [other[c]], weight, weight_pair, waits, BF16)
        arrived.append(swap(after, 2))
    here = project_call(
        channels, [(0, CHUNK)] * chunks, mixed, other, weight, weight_pair, [after], F32
    )
    out = None
    for c in range(chunks):
        out = add_call(c, here, [arrived[c]], out)
    return out


def solution(mesh):
    n_ctx, n_tp = mesh.shape["ctx"], mesh.shape["tp"]
    in_specs = (
        P("ctx", "tp"),
        P("ctx", "tp"),
        P("ctx", "tp"),
        P("tp", None),
        P("tp", None),
        P("tp"),
        P("tp", None),
    )

    def body(*args):
        return shards(*args, n_ctx=n_ctx, n_tp=n_tp)

    return jax.shard_map(body, mesh=mesh, in_specs=in_specs, out_specs=P("ctx", "tp"), check_vma=False)
```

```python
import jax
import jax.numpy as jnp
from jax import lax
from jax.experimental import pallas as pl
from jax.experimental.pallas import tpu as pltpu
from jax.sharding import PartitionSpec as P

GROUP = 16
LANES = 128
BLK = 256
SEG = 256
F32, BF16 = jnp.float32, jnp.bfloat16
VMEM_SPEC = pl.BlockSpec(memory_space=pltpu.VMEM)
HBM_SPEC = pl.BlockSpec(memory_space=pltpu.HBM)
ANY_SPEC = pl.BlockSpec(memory_space=pl.ANY)
PARAMS = pltpu.CompilerParams(vmem_limit_bytes=16 << 20)


COST = pl.CostEstimate(flops=1, bytes_accessed=1, transcendentals=0)


def in_hbm(x):
    return pltpu.with_memory_space_constraint(x, pltpu.HBM)


def shape(dims, dtype=F32):
    return jax.ShapeDtypeStruct(dims, dtype)


def split_bf16(x, parts):
    pieces = []
    for _ in range(parts):
        piece = x.astype(BF16)
        pieces.append(piece)
        x = x - piece.astype(F32)
    return pieces


def dot(a, b):
    return lax.dot_general(a, b, (((1,), (0,)), ((), ())), preferred_element_type=F32)


def group_mask(groups, modes, channels):
    dims = (groups, modes, channels)
    return lax.broadcasted_iota(jnp.int32, dims, 0) == (
        lax.broadcasted_iota(jnp.int32, dims, 2) // GROUP
    )


def column_of(table, first, groups):
    modes, width = table.shape
    rows = groups * modes
    spread = jnp.broadcast_to(table[None], (groups, modes, width)).reshape(rows, width)
    pick = lax.broadcasted_iota(jnp.int32, (rows, width), 1) == (
        lax.broadcasted_iota(jnp.int32, (rows, width), 0) // modes + first
    )
    return jnp.sum(jnp.where(pick, spread, 0.0), axis=1, keepdims=True)


def compact(dense, mask):
    return jnp.sum(jnp.where(mask, dense.reshape(mask.shape), 0.0), axis=0)


def tile_rows(modes, block):
    tiles = BLK // LANES
    for tile in range(tiles):
        at = (block * tiles + tile) * modes
        yield slice(at, at + modes), slice(tile * LANES, (tile + 1) * LANES)


def spread_table(table_ref, out_ref):
    modes, groups = table_ref.shape
    step = BLK // GROUP
    mask = group_mask(step, modes, BLK)
    for block in range(groups // step):
        column = column_of(table_ref[...], block * step, step)
        table = compact(jnp.broadcast_to(column, (step * modes, BLK)), mask)
        for at, lanes in tile_rows(modes, block):
            out_ref[at, :] = table[:, lanes]


def flatten_table(table_ref, out_ref):
    modes, groups = table_ref.shape
    step = BLK // GROUP
    rows = step * modes
    diagonal = lax.broadcasted_iota(jnp.int32, (rows, rows), 0) == lax.broadcasted_iota(
        jnp.int32, (rows, rows), 1
    )
    for block in range(groups // step):
        column = column_of(table_ref[...], block * step, step)
        kept = jnp.where(diagonal, jnp.broadcast_to(column, (rows, rows)), 0.0)
        out_ref[:, block * rows : (block + 1) * rows] = jnp.sum(kept, axis=0, keepdims=True)


def summary_kernel(
    k_hbm, v_hbm, rates_hbm, residues_hbm, skip_hbm,
    sum_ref, sent_ref, rate_ref, u_ref, rates_ref, residues_ref, skip_ref,
    k_ref, v_ref, decay_ref, sems,
):
    tokens, channels = u_ref.shape
    modes = rates_ref.shape[0]
    groups = BLK // GROUP
    rows = groups * modes
    blocks = channels // BLK
    segments = tokens // SEG
    copies = [
        pltpu.make_async_copy(src, dst, sems.at[i])
        for i, (src, dst) in enumerate(
            ((rates_hbm, rates_ref), (residues_hbm, residues_ref), (skip_hbm, skip_ref))
        )
    ]
    small = len(copies)
    for seg in range(segments):
        part = pl.ds(seg * SEG, SEG)
        for src, dst in ((k_hbm, k_ref), (v_hbm, v_ref)):
            sem = sems.at[len(copies)]
            copies.append(pltpu.make_async_copy(src.at[part, :], dst.at[part, :], sem))
    for copy in copies:
        copy.start()
    copies[0].wait()
    mask = group_mask(groups, modes, BLK)
    position = lax.broadcasted_iota(jnp.int32, (rows, LANES), 1).astype(F32)
    for block in range(blocks):
        rate = column_of(rates_ref[...], block * groups, groups)
        part = jnp.exp(-rate * (LANES - 1.0 - position))
        parts = [part]
        for _ in range(1, SEG // LANES):
            part = part * jnp.exp(-rate * float(LANES))
            parts = [part] + parts
        at = 2 * block * rows
        for i, piece in enumerate(split_bf16(jnp.concatenate(parts, axis=1), 2)):
            decay_ref[at + i * rows : at + (i + 1) * rows, :] = piece
        table = compact(jnp.broadcast_to(rate, (rows, BLK)), mask)
        for at, lanes in tile_rows(modes, block):
            rate_ref[at, :] = table[:, lanes]
    for seg in range(segments):
        part = slice(seg * SEG, (seg + 1) * SEG)
        for copy in copies[small + 2 * seg : small + 2 * seg + 2]:
            copy.wait()
        for block in range(blocks):
            lanes = slice(block * BLK, (block + 1) * BLK)
            u = (k_ref[part, lanes].astype(F32) * v_ref[part, lanes].astype(F32)).astype(BF16)
            u_ref[part, lanes] = u
            both = dot(decay_ref[2 * block * rows : (2 * block + 2) * rows, :], u)
            here = compact(both[:rows] + both[rows:], mask)
            for at, lanes in tile_rows(modes, block):
                part_sum = here[:, lanes]
                if seg:
                    part_sum = part_sum + jnp.exp(-rate_ref[at, :] * float(SEG)) * sum_ref[at, :]
                sum_ref[at, :] = part_sum
                if seg == segments - 1:
                    sent_ref[at, :] = part_sum.astype(BF16)
    for copy in copies[1:small]:
        copy.wait()


def summary_call(key_in, value, rates_t, residues_t, skip_tiles):
    tokens, channels = key_in.shape
    modes = rates_t.shape[0]
    table = shape((channels // LANES * modes, LANES))
    return pl.pallas_call(
        summary_kernel,
        in_specs=[HBM_SPEC] * 5,
        out_specs=[VMEM_SPEC] * 7,
        out_shape=[
            table, shape(table.shape, BF16), table,
            shape((tokens, channels), BF16),
            shape(rates_t.shape), shape(residues_t.shape), shape(skip_tiles.shape),
        ],
        scratch_shapes=[
            pltpu.VMEM((tokens, channels), BF16),
            pltpu.VMEM((tokens, channels), BF16),
            pltpu.VMEM((2 * channels // GROUP * modes, SEG), BF16),
            pltpu.SemaphoreType.DMA((3 + 2 * tokens // SEG,)),
        ],
        compiler_params=PARAMS,
        cost_estimate=COST,
        name="block_summary",
    )(*[in_hbm(x) for x in (key_in, value, rates_t, residues_t, skip_tiles)])


def local_kernel(
    begin, count, modes, parts, started, fresh,
    u_in, rate_ref, residue_ref, skip_ref, q_hbm, weight_hbm, table_ref, *rest,
):
    carry_ref = rest[1] if started else None
    out_ref, q_ref, end_ref, *rest = rest[1 + started :]
    u_ref, sems = rest[-2:]
    fresh_ref = rest[-3] if fresh else None
    tiles = u_in.shape[1] // LANES
    rows = slice(begin, begin + count)
    copies = [pltpu.make_async_copy(q_hbm.at[pl.ds(begin, count), :], q_ref, sems.at[0])]
    if parts:
        me = lax.axis_index("tp")
        parts_ref = rest[0]
        depth, width = weight_hbm.shape[0], parts_ref.shape[1]
        for i, part in enumerate(parts):
            src = weight_hbm.at[:, pl.ds(pl.multiple_of((me ^ part) * width, width), width)]
            dst = parts_ref.at[pl.ds(i * depth, depth), :]
            copies.append(pltpu.make_async_copy(src, dst, sems.at[i + 1]))
    for copy in copies:
        copy.start()
    if fresh == "spread":
        spread_table(table_ref, fresh_ref)
        residue_ref = fresh_ref
    elif fresh == "flat":
        flatten_table(table_ref, fresh_ref)
    for tile in range(tiles):
        u = u_in[rows, tile * LANES : (tile + 1) * LANES]
        u_ref[tile * count : (tile + 1) * count, :] = u.astype(F32)
    decay = [jnp.exp(-rate_ref[pl.ds(m, tiles, stride=modes), :]) for m in range(modes)]
    residue = [residue_ref[pl.ds(m, tiles, stride=modes), :] for m in range(modes)]
    skip = skip_ref[...]

    def step(t, states):
        u = u_ref[pl.ds(t, tiles, stride=count), :]
        states = tuple(d * s + u for d, s in zip(decay, states))
        terms = [skip * u] + [r * s for r, s in zip(residue, states)]
        while len(terms) > 1:
            terms = [a + b for a, b in zip(terms[::2], terms[1::2])] + (
                [terms[-1]] if len(terms) % 2 else []
            )
        out_ref[pl.ds(t, tiles, stride=count), :] = terms[0]
        return states

    if started:
        first = tuple(carry_ref[m * tiles : (m + 1) * tiles, :] for m in range(modes))
    else:
        first = (jnp.zeros((tiles, LANES), F32),) * modes
    last = lax.fori_loop(0, count, step, first, unroll=4)
    for m in range(modes):
        end_ref[m * tiles : (m + 1) * tiles, :] = last[m]
    for copy in copies:
        copy.wait()


def local_call(
    begin, count, parts, fresh, u, rate_table, residue_table, skip_tiles, query, weight, table,
    after, carry, width,
):
    channels = u.shape[1]
    tiles = channels // LANES
    modes = rate_table.shape[0] // tiles
    started = carry is not None
    extra = [shape((modes * tiles, LANES))]
    if parts:
        extra.append(shape((len(parts) * channels, width), BF16))
    if fresh:
        extra.append(shape((tiles * modes, LANES) if fresh == "spread" else (1, table.size)))
    return pl.pallas_call(
        lambda *refs: local_kernel(begin, count, modes, parts, started, fresh, *refs),
        in_specs=[VMEM_SPEC] * 4 + [HBM_SPEC] * 2 + [VMEM_SPEC, ANY_SPEC] + [VMEM_SPEC] * started,
        out_specs=[VMEM_SPEC] * (2 + len(extra)),
        out_shape=[shape((count * tiles, LANES)), shape((count, channels), BF16)] + extra,
        scratch_shapes=[
            pltpu.VMEM((tiles * count, LANES), F32),
            pltpu.SemaphoreType.DMA((1 + len(parts),)),
        ],
        compiler_params=PARAMS,
        cost_estimate=COST,
        name="local_conv",
    )(
        u, rate_table, residue_table, skip_tiles, in_hbm(query), in_hbm(weight), table, after,
        *([carry] if started else []),
    )


def join_kernel(span, radix, tokens, started, last, passed_ref, rate_ref, total_ref, *refs):
    rate, total = rate_ref[...], total_ref[...]
    others = [ref[...].astype(F32) for ref in refs[: radix - 1]]
    block = lax.axis_index("ctx")
    digit = (block // span) % radix
    inside = block % span
    state = refs[radix - 1][...] if started else jnp.zeros(rate.shape, F32)

    def decayed(blocks):
        return jnp.exp(-rate * (blocks * tokens).astype(F32))

    if not last:
        total = total * decayed((radix - 1 - digit) * span)
    for k, other in enumerate(others, 1):
        theirs = digit ^ k
        apart = jnp.maximum(digit - 1 - theirs, 0) * span + inside
        state = jnp.where(theirs < digit, state + decayed(apart) * other, state)
        if not last:
            total = total + decayed((radix - 1 - theirs) * span) * other
    refs[-1][...] = state
    if not last:
        refs[-3][...] = total
        refs[-2][...] = total.astype(BF16)


def join_call(span, radix, tokens, last, passed, rate_table, total, others, state):
    started = state is not None
    ends = [] if last else [shape(total.shape), shape(total.shape, BF16)]
    return pl.pallas_call(
        lambda *refs: join_kernel(span, radix, tokens, started, last, *refs),
        in_specs=[ANY_SPEC] + [VMEM_SPEC] * (1 + radix + started),
        out_specs=[ANY_SPEC] + [VMEM_SPEC] * (1 + len(ends)),
        out_shape=[shape(passed.shape, passed.dtype), *ends, shape(total.shape)],
        input_output_aliases={0: 0},
        compiler_params=PARAMS,
        cost_estimate=COST,
        name="join_blocks",
    )(passed, rate_table, total, *others, *([state] if started else []))


def mix_kernel(begin, modes, parts, outs, residue_ref, flat_ref, state_ref, *refs):
    count = len(parts)
    pieces, out_refs = list(zip(refs[: 2 * count : 2], refs[1 : 2 * count : 2])), refs[-outs:]
    groups = BLK // GROUP
    tiles = BLK // LANES
    rows = groups * modes
    tokens = sum(ref.shape[0] for ref in out_refs)
    mask = group_mask(groups, modes, BLK)
    since = lax.broadcasted_iota(jnp.int32, (tokens, rows), 0).astype(F32) + (begin + 1.0)
    for block in range(out_refs[0].shape[1] // BLK):
        tile0 = block * tiles
        weighted = [
            state_ref[i * modes : (i + 1) * modes, :] * residue_ref[i * modes : (i + 1) * modes, :]
            for i in range(tile0, tile0 + tiles)
        ]
        spread = jnp.broadcast_to(jnp.concatenate(weighted, axis=1)[None], (groups, modes, BLK))
        spread = jnp.where(mask, spread, 0.0).reshape(rows, BLK)
        flat = flat_ref[:, block * rows : (block + 1) * rows]
        decay_hi, decay_lo = split_bf16(jnp.exp(-flat * since), 2)
        state_hi, state_lo = split_bf16(spread, 2)
        past = dot(decay_lo, state_hi) + dot(decay_hi, state_lo) + dot(decay_hi, state_hi)
        at = 0
        for (q_ref, local_ref), (start, stop) in zip(pieces, parts):
            count = stop - start
            for tile in range(tiles):
                lanes = slice((tile0 + tile) * LANES, (tile0 + tile + 1) * LANES)
                row = (tile0 + tile) * q_ref.shape[0] + start
                conv = local_ref[row : row + count, :]
                conv = conv + past[at : at + count, tile * LANES : (tile + 1) * LANES]
                mixed = (q_ref[start:stop, lanes].astype(F32) * conv).astype(BF16)
                first = 0
                for out_ref in out_refs:
                    last = first + out_ref.shape[0]
                    lo, hi = max(first, at), min(last, at + count)
                    if lo < hi:
                        out_ref[lo - first : hi - first, lanes] = mixed[lo - at : hi - at]
                    first = last
            at += count


def mix_call(begin, sizes, parts, query, local, residue_table, flat_rates, state, after):
    channels = query[0].shape[1]
    modes = flat_rates.shape[1] * GROUP // channels
    pieces = [x for pair in zip(query, local) for x in pair]
    return pl.pallas_call(
        lambda *refs: mix_kernel(begin, modes, parts, len(sizes), *refs),
        in_specs=[VMEM_SPEC] * (3 + len(pieces)) + [ANY_SPEC] * len(after),
        out_specs=[VMEM_SPEC] * len(sizes),
        out_shape=[shape((size, channels), BF16) for size in sizes],
        compiler_params=PARAMS,
        cost_estimate=COST,
        name="mix",
    )(residue_table, flat_rates, state, *pieces, *after)


def project_kernel(row, count, own_w_ref, pair_w_ref, *refs):
    cols = 256
    own_refs, pair_refs, out_ref = refs[:count], refs[count : 2 * count], refs[-1]
    rows_w = slice(row, row + own_refs[0].shape[1])
    for first in range(0, out_ref.shape[1], cols):
        lanes = slice(first, first + cols)
        at = 0
        for own, pair in zip(own_refs, pair_refs):
            total = dot(own[...], own_w_ref[:, lanes]) + dot(pair[...], pair_w_ref[rows_w, lanes])
            out_ref[at : at + own.shape[0], lanes] = total.astype(out_ref.dtype)
            at += own.shape[0]


def project_call(row, mixed, mixed_pair, weight, weight_pair, after, out_dtype):
    return pl.pallas_call(
        lambda *refs: project_kernel(row, len(mixed), *refs),
        in_specs=[VMEM_SPEC] * (2 + 2 * len(mixed)) + [ANY_SPEC] * len(after),
        out_specs=VMEM_SPEC,
        out_shape=shape((sum(x.shape[0] for x in mixed), weight.shape[1]), out_dtype),
        compiler_params=PARAMS,
        cost_estimate=COST,
        name="project",
    )(weight, weight_pair, *mixed, *mixed_pair, *after)


def add_kernel(begin, first, near_ref, arrived_ref, *refs):
    out_hbm, rows_ref, sems = refs[-3:]
    count, width = rows_ref.shape
    halves = sems.shape[0]
    copies = []
    for half in range(halves):
        rows = slice(half * count // halves, (half + 1) * count // halves)
        size = rows.stop - rows.start
        near = near_ref[first + rows.start : first + rows.stop, :]
        rows_ref[rows, :] = (near + arrived_ref[rows, :].astype(F32)).astype(BF16)
        copies.append(
            pltpu.make_async_copy(
                rows_ref.at[pl.ds(rows.start, size), :],
                out_hbm.at[pl.ds(begin + rows.start, size), :],
                sems.at[half],
            )
        )
        copies[-1].start()
    for copy in copies:
        copy.wait()


def add_call(begin, near, first, arrived, out, tokens):
    count, width = arrived.shape
    started = out is not None
    return pl.pallas_call(
        lambda *refs: add_kernel(begin, first, *refs),
        in_specs=[VMEM_SPEC] * 2 + [HBM_SPEC] * started,
        out_specs=HBM_SPEC,
        out_shape=shape((tokens, width), BF16),
        input_output_aliases={2: 0} if started else {},
        scratch_shapes=[pltpu.VMEM((count, width), BF16), pltpu.SemaphoreType.DMA((2,))],
        compiler_params=PARAMS,
        cost_estimate=COST,
        name="add_arrived",
    )(near, arrived, *([out] if started else []))


def shards(query, key_in, value, rates, residues, skip_gain, out_weight, *, n_ctx, n_tp):
    tokens, channels = query.shape
    width = out_weight.shape[1] // n_tp

    def swap(x, bit):
        return lax.ppermute(x, "tp", [(i, i ^ bit) for i in range(n_tp)])

    skip_tiles = skip_gain.reshape(channels // LANES, LANES)
    total, sent, rate_table, u, rates_t, residues_t, skip_tiles = summary_call(
        key_in, value, rates.T, residues.T, skip_tiles
    )
    unit = tokens // 32
    sizes = [10 * unit, 9 * unit, 13 * unit]
    begins = [0, sizes[0], sizes[0] + sizes[1]]
    mixes = [[8 * unit], [6 * unit] * 2, [4 * unit] * 3]
    transfers = [1, 2, 2, 1]
    local, q, extras = [], [], []

    def next_local(after, carry):
        index = len(local)
        parts = ((3, 1), (2,), (0,))[index]
        fresh = ("spread", "flat", None)[index]
        residue_table = extras[1] if index else rate_table
        out, q_rows, end, *got = local_call(
            begins[index], sizes[index], parts, fresh, u, rate_table, residue_table, skip_tiles,
            query, out_weight, rates_t if index else residues_t, after, carry, width,
        )
        local.append(out)
        q.append(q_rows)
        extras.extend(got)
        return end

    state = carry = weight_pair = None
    span = 1
    while span < n_ctx:
        radix = 2
        others = [
            lax.ppermute(sent, "ctx", [(i, i ^ (k * span)) for i in range(n_ctx)])
            for k in range(radix - 1, 0, -1)
        ][::-1]
        if len(local) < len(sizes):
            carry = next_local(total, carry)
        last = span * radix == n_ctx
        passed = extras[0] if span == 1 else carry
        passed, *ends, state = join_call(
            span, radix, tokens, last, passed, rate_table, total, others, state
        )
        if span == 1:
            weight_pair = swap(passed, 1)
        else:
            carry = passed
        if not last:
            total, sent = ends
        span *= radix
    while len(local) < len(sizes):
        carry = next_local(carry, carry)
    residue_table, weight_far, flat_rates, weight_near = extras[1:]

    def mix(index, after):
        begin = sum(sum(m) for m in mixes[:index])
        end = begin + sum(mixes[index])
        used = [
            (i, (max(begin - at, 0), min(end - at, size)))
            for i, (at, size) in enumerate(zip(begins, sizes))
            if at < end and at + size > begin
        ]
        mixed = mix_call(
            begin, mixes[index], [part for _, part in used], [q[i] for i, _ in used],
            [local[i] for i, _ in used], residue_table, flat_rates, state, after,
        )
        return mixed, [swap(x, 1) for x in mixed]

    def send(own, other, after):
        part = project_call(0, own, other, weight_far, weight_pair, after, BF16)
        arrived.append(swap(part, 2))
        return part

    def keep(own, other, after):
        near.append(project_call(channels, own, other, weight_near, weight_pair, after, F32))
        return near[-1]

    arrived, near = [], []
    own0, other0 = mix(0, [carry])
    own1, other1 = mix(1, own0)
    far = send(own0, other0, own1[-1:])
    here = keep(own0, other0, [far])
    far = send(own1, other1, [here])
    here = keep(own1, other1, [far])
    own2, other2 = mix(2, [here, arrived[0]])
    far = own2[-1]
    done = 0
    for count in transfers[2:]:
        part = slice(done, done + count)
        far = send(own2[part], other2[part], [far])
        done += count
    keep(own2, other2, [far])
    out = None
    begin = 0
    for i, piece in enumerate(arrived):
        part = min(i, 2)
        first = begin - sum(x.shape[0] for x in near[:part])
        out = add_call(begin, near[part], first, piece, out, tokens)
        begin += piece.shape[0]
    return out


def solution(mesh):
    n_ctx, n_tp = mesh.shape["ctx"], mesh.shape["tp"]
    in_specs = (
        P("ctx", "tp"),
        P("ctx", "tp"),
        P("ctx", "tp"),
        P("tp", None),
        P("tp", None),
        P("tp"),
        P("tp", None),
    )

    def body(*args):
        return shards(*args, n_ctx=n_ctx, n_tp=n_tp)

    return jax.shard_map(body, mesh=mesh, in_specs=in_specs, out_specs=P("ctx", "tp"), check_vma=False)
```
